32 devices in a mesh: expert: 16 (over z, x, core), shard: 2 (over y).
Axes of the slice: x: 2, y: 2, z: 4, core: 2. Of those that a mesh axis runs over, the one named last changes fastest.
Arguments:
- tokens: bfloat16 [640, 4096], P('expert'), may hold values from -6 to 6
- expert_ids: int32 [640, 8], P('expert'), may hold values from 0 to 15, all different within a row; in each aligned block of 40 rows (0 to 39, 40 to 79, ...) at most 40 rows name the same one
- route_weights: float32 [640, 8], P('expert'), may hold values from 0.05 to 0.5
- partner: int32 [16], replicated, may hold values from 0 to 15, as said below
- gate_up: bfloat16 [16, 2, 768, 4096], P('expert', None, 'shard'), may hold values from -0.09375 to 0.09375
- down_weight: bfloat16 [16, 768, 4096], P('expert', None, 'shard'), may hold values from -0.21875 to 0.21875
- down_grad: bfloat16 [16, 128, 4096], P('expert', None, 'shard'), may hold values from -6 to 6
- moment_one: float32 [16, 128, 4096], P('expert', None, 'shard'), may hold values from -6 to 6
- moment_two: float32 [16, 128, 4096], P('expert', None, 'shard'), may hold values from 0.3 to 3
Outputs:
- combined: bfloat16 [640, 4096], P('expert', 'shard')
- trained_rows: bfloat16 [16, 128, 4096], P('expert', None, 'shard')
- first_moment: float32 [16, 128, 4096], P('expert', None, 'shard')
- second_moment: float32 [16, 128, 4096], P('expert', None, 'shard')
The draws below stay inside these ranges and needn't reach their ends.
Inputs may be any that keep to these rules, and one draw needn't show every extreme that they name: `expert_ids`: each row names 8 different experts. In each aligned block of 40 rows (the rows held by one index of expert) no expert is named by more than 40 rows, a bound that some block reaches. partner[partner[p]] = p and partner[p] != p for every p: the list splits all 16 indices into pairs.
All inputs are finite; a program needn't handle non-finite values.
Results may differ from the reference program's by a relative error of at most 0.0058.
Values may be sent and summed in bfloat16 or wider, within the bound.
A program may use at most 64 MiB of HBM per device.

```python
import math
import jax
import jax.numpy as jnp
import numpy as np
from jax import lax

D = 4096
FF = 768
HOT = 128
TOP = 8
STEP = 100
TOK_E = 40
EXPERTS = 16
CAP = 40
TOKENS = 640
N_EXPERT = 16


def draw_partner(key, part):
    order = jax.random.permutation(key, EXPERTS).astype(jnp.int32)
    paired = order.reshape(EXPERTS // 2, 2)
    swapped = jnp.stack([paired[:, 1], paired[:, 0]], axis=1).reshape(EXPERTS)
    return jnp.zeros((EXPERTS,), jnp.int32).at[order].set(swapped)


def shard_levels(own_key, dims, shards, smallest, top_value):
    loudness, own = 1.0, jax.random.fold_in(own_key, 6)
    for dim, parts in shards:
        steps = jnp.exp(jax.random.uniform(jax.random.fold_in(own, dim), (parts,), jnp.float32, smallest / len(shards), top_value / len(shards)))
        loudness = loudness * jnp.repeat(steps, dims[dim] // parts).reshape([-1 if axis == dim else 1 for axis in range(len(dims))])
    return loudness


def assign_block(stream_key, own, number, rows, amount, top, most, skew):
    ranking = jax.random.permutation(stream_key, amount)
    heavy_load, common = shares(amount, rows * top, most, skew, True), shares(amount, rows * top, most, skew, False)
    places = jnp.arange(amount)

    def named(tallies, turn):
        used = int((tallies > 0).sum())
        fixed = max(1, used // 4)
        shifted = fixed + (places - fixed + turn * (used - fixed)) % max(1, amount - fixed)
        return jnp.zeros((amount,), jnp.int32).at[ranking[jnp.where(places < fixed, places, shifted)]].set(jnp.asarray(tallies, jnp.int32))

    tallies = jnp.where(number % 4 == 0, named(heavy_load, number // 4), named(common, number - number // 4 - 1))
    mixed = jax.random.permutation(jax.random.fold_in(own, 3), amount)
    donor, receiver = mixed[0:amount // 2 * 2:2], mixed[1:amount // 2 * 2:2]
    margin = jnp.minimum(tallies[donor] - 1, most - tallies[receiver]) // 2
    margin = jnp.where((donor == ranking[0]) | (receiver == ranking[0]) | (tallies[receiver] == 0), 0, jnp.maximum(margin, 0))
    shifted = jax.random.randint(jax.random.fold_in(own, 4), (amount // 2,), 0, 1 << 20) % (margin + 1)
    tallies = tallies.at[donor].add(-shifted).at[receiver].add(shifted)
    items = jnp.searchsorted(jnp.cumsum(tallies), jnp.arange(rows * top), side="right").astype(jnp.int32)
    grid = items.reshape(top, rows).T
    grid = grid[jax.random.permutation(jax.random.fold_in(own, 1), rows)]
    turn = jax.random.randint(jax.random.fold_in(own, 2), (rows, 1), 0, top)
    return jnp.take_along_axis(grid, (jnp.arange(top)[None, :] + turn) % top, axis=1)


def shares(number_of, total, reach, skew, full):
    loads = [(1 << 20) // math.isqrt(standing ** skew) + 1 for standing in range(1, number_of + 1)]
    largest = reach if full else min(reach, max(-(-total // number_of), total * loads[0] // sum(loads)))
    least = 1 if total - largest >= number_of - 1 else 0
    given, rest = [largest] + [least] * (number_of - 1), total - largest - least * (number_of - 1)
    while rest > 0:
        movable = [i for i in range(1, number_of) if given[i] < largest] or [i for i in range(1, number_of) if given[i] < reach]
        mass, left = sum([loads[i] for i in movable]), rest
        for i in movable:
            extra = min(reach - given[i], max(1, left * loads[i] // mass), rest)
            given[i] = given[i] + extra
            rest = rest - extra
    return np.array(given)


def gaussian(key, dims, width, bound, split=(), held_as=jnp.bfloat16):
    result = width * jax.random.normal(key, dims, jnp.float32)
    if split:
        result = result * shard_levels(key, dims, split, -0.22, 0.18)
    return jnp.clip(result, -bound, bound).astype(held_as)


def setup_inputs(seed: int = 0) -> dict:
    key_list = jax.random.split(jax.random.key(seed), 10)
    tokens = gaussian(key_list[0], (TOKENS, D), 1.0, 6.0, ((0, 16),))
    expert_ids_keys = jax.random.split(jax.random.fold_in(key_list[1], 1), TOKENS // TOK_E)
    expert_ids_turns = jax.random.permutation(jax.random.fold_in(key_list[1], 3), TOKENS // TOK_E)
    expert_ids = jax.vmap(lambda own, number: assign_block(jax.random.fold_in(key_list[1], 2), own, number, TOK_E, EXPERTS, TOP, CAP, 2))(expert_ids_keys, expert_ids_turns).reshape((TOKENS, TOP))
    route_weights = jnp.clip(jnp.exp(math.log(0.5) - 2.3025851 * jax.random.uniform(key_list[2], (TOKENS, TOP), jnp.float32) ** shard_levels(key_list[2], (TOKENS, TOP), ((0, 16),), -0.2, 0.2)), 0.05, 0.5)
    partner = draw_partner(jax.random.fold_in(key_list[9], 71), 0)
    gate_up = gaussian(key_list[4], (EXPERTS, 2, FF, D), D ** -0.5, 0.09375, ((0, 16), (2, 2)))
    down_weight = gaussian(key_list[5], (EXPERTS, FF, D), FF ** -0.5, 0.21875, ((0, 16), (2, 2)))
    down_grad = gaussian(key_list[6], (EXPERTS, HOT, D), 1.0, 6.0, ((0, 16), (2, 2)))
    moment_one = gaussian(key_list[7], (EXPERTS, HOT, D), 1.0, 6.0, ((0, 16), (2, 2)), jnp.float32)
    moment_two = jnp.clip(jnp.exp(math.log(3.0) - 2.3025851 * jax.random.uniform(key_list[8], (EXPERTS, HOT, D), jnp.float32) ** shard_levels(key_list[8], (EXPERTS, HOT, D), ((0, 16), (2, 2)), -0.2, 0.2)), 0.3, 3.0)
    return {"tokens": tokens, "expert_ids": expert_ids, "route_weights": route_weights, "partner": partner, "gate_up": gate_up, "down_weight": down_weight, "down_grad": down_grad, "moment_one": moment_one, "moment_two": moment_two}


learn_rate = 0.01
beta_one = 0.9
beta_two = 0.999
epsilon = 1e-08
decay_rate = 0.1

def adamw(weight, gradient, first, second):
    grad_wide = gradient.astype(jnp.float32)
    first_new = beta_one * first + (1.0 - beta_one) * grad_wide
    second_new = beta_two * second + (1.0 - beta_two) * grad_wide * grad_wide
    first_hat = first_new / (1.0 - beta_one ** STEP)
    second_hat = second_new / (1.0 - beta_two ** STEP)
    weight_wide = weight.astype(jnp.float32)
    updated = weight_wide - learn_rate * (first_hat / (jnp.sqrt(second_hat) + epsilon) + decay_rate * weight_wide)
    return (updated.astype(jnp.bfloat16), first_new, second_new)

def expert_rows(token_rows, gate_one, down_one):
    hidden_count = gate_one.shape[1]
    joined = gate_one.reshape(2 * hidden_count, gate_one.shape[2])
    projected = jnp.dot(token_rows, joined.T, preferred_element_type=jnp.float32)
    hidden = (jax.nn.silu(projected[:, :hidden_count]) * projected[:, hidden_count:]).astype(jnp.bfloat16)
    return jnp.dot(hidden, down_one, preferred_element_type=jnp.float32).astype(jnp.bfloat16)

def reference(tokens, expert_ids, route_weights, partner, gate_up, down_weight, down_grad, moment_one, moment_two):
    new_rows, first_new, second_new = adamw(down_weight[:, :HOT], down_grad, moment_one, moment_two)
    down_full = jnp.concatenate([new_rows, down_weight[:, HOT:]], axis=1)
    per_expert = N_EXPERT * CAP
    blocks = TOKENS // TOK_E
    assigned = expert_ids.reshape(blocks, TOK_E * TOP).astype(jnp.int32)
    experts = jnp.arange(EXPERTS, dtype=jnp.int32)
    picked = (assigned[:, :, None] == experts[None, None, :]).astype(jnp.int32)
    running = jnp.cumsum(picked, axis=1)
    rank_in_block = lax.optimization_barrier(jnp.sum((running - 1) * picked, axis=2))
    block_index = jnp.arange(blocks, dtype=jnp.int32)[:, None]
    slot_keys = (assigned * per_expert + block_index * CAP + rank_in_block).reshape(-1).astype(jnp.int32)
    token_index = jnp.repeat(jnp.arange(TOKENS, dtype=jnp.int32), TOP)
    slot_tokens = jnp.full((EXPERTS * per_expert,), TOKENS, jnp.int32).at[slot_keys].set(token_index).reshape(EXPERTS, per_expert)
    slot_weights = jnp.zeros((EXPERTS * per_expert,), jnp.float32).at[slot_keys].set(route_weights.reshape(-1).astype(jnp.float32)).reshape(EXPERTS, per_expert)
    padded = jnp.concatenate([tokens, jnp.zeros((1, D), jnp.bfloat16)], axis=0)

    def one_expert(summed, inputs):
        token_slots, weight_slots, gate_one, down_one = inputs
        outputs = expert_rows(padded[token_slots], gate_one, down_one)
        return (summed.at[token_slots].add(weight_slots[:, None] * outputs.astype(jnp.float32)), None)
    summed, unused = lax.scan(one_expert, jnp.zeros((TOKENS + 1, D), jnp.float32), (slot_tokens, slot_weights, gate_up, down_full))
    combined = summed[:TOKENS].astype(jnp.bfloat16)
    return (combined, new_rows[partner], first_new[partner], second_new[partner])
```

```python
import jax
import jax.numpy as jnp
from jax import lax
from jax.sharding import PartitionSpec as P

STEP = 100


learn_rate = 0.01
beta_one = 0.9
beta_two = 0.999
epsilon = 1e-08
decay_rate = 0.1


def adamw(weight, gradient, first, second):
    grad_wide = gradient.astype(jnp.float32)
    first_new = beta_one * first + (1.0 - beta_one) * grad_wide
    second_new = beta_two * second + (1.0 - beta_two) * grad_wide * grad_wide
    first_hat = first_new / (1.0 - beta_one**STEP)
    second_hat = second_new / (1.0 - beta_two**STEP)
    weight_wide = weight.astype(jnp.float32)
    updated = weight_wide - learn_rate * (
        first_hat / (jnp.sqrt(second_hat) + epsilon) + decay_rate * weight_wide
    )
    return (updated.astype(jnp.bfloat16), first_new, second_new)


def relocate(payload, partner):
    groups = lax.axis_size("expert")
    me = lax.axis_index("expert")

    def exchange(distance):
        pairs = [(i, i ^ distance) for i in range(groups)]
        return lambda block: lax.ppermute(block, "expert", pairs)

    offset = lax.bitwise_xor(me, partner[me])
    return lax.switch(offset - 1, [exchange(d) for d in range(1, groups)], payload)


def shards(
    tokens,
    expert_ids,
    route_weights,
    partner,
    gate_up,
    down_weight,
    down_grad,
    moment_one,
    moment_two,
):
    groups = lax.axis_size("expert")
    token_count = tokens.shape[0]
    model_width = tokens.shape[1]
    part_width = down_weight.shape[2]
    trained = down_grad.shape[1]
    capacity = 2 * token_count * expert_ids.shape[1] // groups
    new_rows, first_new, second_new = adamw(
        down_weight[:, :trained], down_grad, moment_one, moment_two
    )
    down_new = jnp.concatenate([new_rows, down_weight[:, trained:]], axis=1)
    wide = jnp.concatenate(
        [new_rows, first_new.astype(jnp.bfloat16), second_new.astype(jnp.bfloat16)], axis=0
    )
    arrived = relocate(wide, partner)
    rows_out = arrived[0:1]
    first_out = arrived[1:2].astype(jnp.float32)
    second_out = arrived[2:3].astype(jnp.float32)
    experts = jnp.arange(groups, dtype=jnp.int32)
    picked = (expert_ids[:, :, None] == experts[None, None, :]).astype(jnp.int32)
    running = jnp.cumsum(picked.reshape(-1, groups), axis=0).reshape(picked.shape)
    slot_index = jnp.sum((running - 1) * picked, axis=2)
    position = expert_ids * capacity + slot_index
    positions = jnp.arange(groups * capacity, dtype=jnp.int32)
    matches = position[None, :, :] == positions[:, None, None]
    dispatch = jnp.sum(matches.astype(jnp.int32), axis=2).astype(jnp.bfloat16)
    weighting = jnp.sum(jnp.where(matches, route_weights[None, :, :], 0.0), axis=2)
    outgoing = jnp.dot(dispatch, tokens, preferred_element_type=jnp.float32).astype(jnp.bfloat16)
    outgoing = outgoing.reshape(groups, capacity, tokens.shape[1])
    joined = gate_up.reshape(-1, model_width)
    hidden_count = joined.shape[0] // 2
    down_rows = down_new.reshape(-1, part_width)
    received = lax.all_to_all(outgoing, "expert", split_axis=0, concat_axis=0, tiled=True)
    leading = received.shape[:2]
    token_rows = received.reshape(-1, model_width)
    projected = lax.dot_general(
        token_rows, joined, (((1,), (1,)), ((), ())), preferred_element_type=jnp.float32
    )
    hidden = (jax.nn.silu(projected[:, :hidden_count]) * projected[:, hidden_count:]).astype(
        jnp.bfloat16
    )
    summed = jnp.dot(
        lax.all_gather(hidden, "shard", axis=1, tiled=True),
        down_rows,
        preferred_element_type=jnp.float32,
    )
    results = summed.astype(jnp.bfloat16).reshape(leading + (part_width,))
    returned = lax.all_to_all(results, "expert", split_axis=0, concat_axis=0, tiled=True)
    returned_wide = returned.reshape(-1, part_width).astype(jnp.float32)
    combined = jnp.dot(
        weighting.T,
        returned_wide,
        precision=lax.Precision.HIGHEST,
        preferred_element_type=jnp.float32,
    ).astype(jnp.bfloat16)
    return (combined, rows_out, first_out, second_out)


def solution(mesh):
    return jax.shard_map(
        shards,
        mesh=mesh,
        in_specs=(
            P("expert", None),
            P("expert", None),
            P("expert", None),
            P(),
            P("expert", None, "shard", None),
            P("expert", None, "shard"),
            P("expert", None, "shard"),
            P("expert", None, "shard"),
            P("expert", None, "shard"),
        ),
        out_specs=(
            P("expert", "shard"),
            P("expert", None, "shard"),
            P("expert", None, "shard"),
            P("expert", None, "shard"),
        ),
        check_vma=False,
    )
```

```python
import functools

import jax
import jax.numpy as jnp
from jax import lax
from jax.experimental import pallas as pl
from jax.experimental.pallas import tpu as pltpu
from jax.sharding import PartitionSpec as P

STEP = 100


learn_rate = 0.01
beta_one = 0.9
beta_two = 0.999
epsilon = 1e-08
decay_rate = 0.1


def adamw(weight, gradient, first, second):
    grad_wide = gradient.astype(jnp.float32)
    first_new = beta_one * first + (1.0 - beta_one) * grad_wide
    second_new = beta_two * second + (1.0 - beta_two) * grad_wide * grad_wide
    first_hat = first_new / (1.0 - beta_one**STEP)
    second_hat = second_new / (1.0 - beta_two**STEP)
    weight_wide = weight.astype(jnp.float32)
    updated = weight_wide - learn_rate * (
        first_hat / (jnp.sqrt(second_hat) + epsilon) + decay_rate * weight_wide
    )
    return (updated.astype(jnp.bfloat16), first_new, second_new)


def relocate(payload, partner):
    groups = lax.axis_size("expert")
    me = lax.axis_index("expert")

    def exchange(distance):
        pairs = [(i, i ^ distance) for i in range(groups)]
        return lambda block: lax.ppermute(block, "expert", pairs)

    offset = lax.bitwise_xor(me, partner[me])
    return lax.switch(offset - 1, [exchange(d) for d in range(1, groups)], payload)


MESH_ID = pl.DeviceIdType.MESH
LANES = 128


def moe_kernel(A, B, S, rows, width, tok_ref, gate_ref, down_ref, new_ref, out_ref,
               slab, tok, gate, down, hid, part, got_core, acc, got_b, fin_in, got_a, tail_out, tail_in,
               local_sem, slab_s, slab_r, a_s, a_r, b_s, b_r, c_s, c_r, h_s, h_r,
               pc_s, pc_r, pb_s, pb_r, pa_s, pa_r, t_s, t_r):
    e = lax.axis_index("expert")
    y = lax.axis_index("shard")
    c = lax.rem(e, 2)
    chip = e // 2
    b = lax.rem(chip, B)
    a = chip // B
    half = tok.shape[2] // 2
    pair = 2 * rows
    units = hid.shape[3]
    cols = part.shape[2]
    hc = cols // 2
    trained = new_ref.shape[0]

    def expert_of(a1, b1, c1):
        return (a1 * B + b1) * 2 + c1

    def send(src, dst, ss, rs, target):
        copy = pltpu.make_async_remote_copy(
            src_ref=src, dst_ref=dst, send_sem=ss, recv_sem=rs,
            device_id=target, device_id_type=MESH_ID)
        copy.start()
        return copy

    def landed(dst, rs):
        pltpu.make_async_remote_copy(
            src_ref=dst, dst_ref=dst, send_sem=rs, recv_sem=rs,
            device_id=(expert_of(a, b, 1 - c), y), device_id_type=MESH_ID).wait_recv()

    loads = [
        pltpu.make_async_copy(gate_ref, gate, local_sem.at[0]),
        pltpu.make_async_copy(down_ref.at[pl.ds(trained, down.shape[0] - trained)],
                              down.at[pl.ds(trained, down.shape[0] - trained)], local_sem.at[1]),
        pltpu.make_async_copy(new_ref, down.at[pl.ds(0, trained)], local_sem.at[2]),
    ]
    for load in loads:
        load.start()

    core_dev = (expert_of(a, b, 1 - c), y)
    a_dev = [None] + [(expert_of(lax.rem(a + k, A), b, c), y) for k in range(1, A)]
    b_dev = [None] + [(expert_of(a, lax.rem(b + k, B), c), y) for k in range(1, B)]
    s_dev = [None] + [(e, lax.rem(y + k, S)) for k in range(1, S)]
    barrier = pltpu.get_barrier_semaphore()
    everyone = [core_dev] + a_dev[1:] + b_dev[1:] + s_dev[1:]
    for dev in everyone:
        pl.semaphore_signal(barrier, inc=1, device_id=dev, device_id_type=MESH_ID)
    pl.semaphore_wait(barrier, len(everyone))

    pending = [send(tok_ref, slab, slab_s, slab_r, core_dev)]
    landed(slab, slab_r)
    mine = tok_ref[...].astype(jnp.float32)
    other = slab[...].astype(jnp.float32)
    first = c == 0
    block = jnp.concatenate([jnp.where(first, mine, other), jnp.where(first, other, mine)], axis=0)

    def block_rows(k):
        return pl.ds(pl.multiple_of(lax.rem(a + k, A) * pair, 16), pair)

    my_cols = pl.ds(pl.multiple_of(c * half, LANES), half)
    peer_cols = pl.ds(pl.multiple_of((1 - c) * half, LANES), half)
    tok[b, block_rows(0), :] = block.astype(jnp.bfloat16)

    own = tok.at[b, block_rows(0), my_cols]
    for j in range(1, B):
        pending.append(send(own, own, b_s.at[j, 0], b_r.at[j, 0], b_dev[j]))
    for k in range(1, A):
        pending.append(send(own, own, a_s.at[k], a_r.at[k], a_dev[k]))
    for k in range(1, A):
        piece = tok.at[b, block_rows(A - k), my_cols]
        landed(piece, a_r.at[k])
        for j in range(1, B):
            pending.append(send(piece, piece, b_s.at[j, k], b_r.at[j, k], b_dev[j]))
        pending.append(send(piece, piece, c_s.at[0, k], c_r.at[0, k], core_dev))
    for k in range(1, A):
        landed(tok.at[b, block_rows(A - k), peer_cols], c_r.at[0, k])
    for load in loads:
        load.wait()

    def project(j):
        bj = lax.rem(b + B - j, B)
        x = tok[bj, :, :width]
        both = lax.dot_general(x, gate[...], (((1,), (1,)), ((), ())), preferred_element_type=jnp.float32)
        g = both[:, :units]
        hid[bj, y] = (g / (1.0 + jnp.exp(-g)) * both[:, units:]).astype(jnp.bfloat16)
        piece = hid.at[bj, y]
        for s in range(1, S):
            pending.append(send(piece, piece, h_s.at[j, s], h_r.at[j, s], s_dev[s]))

    def finish(j):
        bj = lax.rem(b + B - j, B)
        for s in range(1, S):
            landed(hid.at[bj, lax.rem(y + S - s, S)], h_r.at[j, s])
        total = jnp.dot(hid[bj, 0], down[pl.ds(0, units), :], preferred_element_type=jnp.float32)
        for s in range(1, S):
            total += jnp.dot(hid[bj, s], down[pl.ds(s * units, units), :], preferred_element_type=jnp.float32)
        lanes = lax.broadcasted_iota(jnp.int32, (A * pair, LANES), 1)
        high = tok[bj, :, width:width + LANES].astype(jnp.float32)
        low = tok[bj, :, width + LANES:width + 2 * LANES].astype(jnp.float32)
        weight = jnp.sum(jnp.where(lanes == e, high + low, 0.0), axis=1, keepdims=True)
        part[bj] = (total * weight).astype(jnp.bfloat16)
        pending.append(send(part.at[bj, :, pl.ds(pl.multiple_of((1 - c) * hc, LANES), hc)],
                            got_core.at[bj], pc_s.at[j], pc_r.at[j], core_dev))

    def join(j):
        bj = lax.rem(b + B - j, B)
        landed(got_core.at[bj], pc_r.at[j])
        acc[j] = (part[bj, :, pl.ds(pl.multiple_of(c * hc, LANES), hc)].astype(jnp.float32)
                  + got_core[bj].astype(jnp.float32)).astype(jnp.bfloat16)
        if j:
            for k in range(A):
                src = acc.at[j, block_rows((k + 1) % A)]
                dst = got_b.at[j, block_rows((k + 1) % A)]
                pending.append(send(src, dst, pb_s.at[j, k], pb_r.at[j, k], b_dev[B - j]))

    project(0)
    for j in range(1, B):
        for k in range(A):
            landed_rows = block_rows(A - k)
            piece = tok.at[lax.rem(b + B - j, B), landed_rows, my_cols]
            landed(piece, b_r.at[j, k])
            pending.append(send(piece, piece, c_s.at[j, k], c_r.at[j, k], core_dev))
        if j == 1:
            finish(0)
        for k in range(A):
            landed(tok.at[lax.rem(b + B - j, B), block_rows(A - k), peer_cols], c_r.at[j, k])
        project(j)
        if j == 1:
            join(0)
        finish(j)
        join(j)
    final = None
    for k in range(A):
        where = block_rows((k + 1) % A)
        total = acc[0, where, :].astype(jnp.float32)
        for j in range(1, B):
            landed(got_b.at[j, where], pb_r.at[j, k])
            total += got_b[j, where, :].astype(jnp.float32)
        if k < A - 1:
            fin_in[k + 1] = total.astype(jnp.bfloat16)
            pending.append(send(fin_in.at[k + 1], got_a.at[k + 1], pa_s.at[k + 1], pa_r.at[k + 1], a_dev[k + 1]))
        else:
            final = total
    for k in range(1, A):
        landed(got_a.at[k], pa_r.at[k])
        final += got_a[k].astype(jnp.float32)
    low_rows, high_rows = final[:rows], final[rows:]
    tail_out[...] = jnp.where(first, high_rows, low_rows).astype(jnp.bfloat16)
    pending.append(send(tail_out, tail_in, t_s, t_r, core_dev))
    out_ref[:, pl.ds(pl.multiple_of(c * hc, LANES), hc)] = jnp.where(first, low_rows, high_rows).astype(jnp.bfloat16)
    landed(tail_in, t_r)
    out_ref[:, pl.ds(pl.multiple_of((1 - c) * hc, LANES), hc)] = tail_in[...]
    for copy in pending:
        copy.wait_send()


def experts_layer(tokens, weighting, gate_up, down_weight, new_rows):
    groups = lax.axis_size("expert")
    S = lax.axis_size("shard")
    rows, width = tokens.shape
    B = groups // 8
    A = 4
    hidden_units, cols = down_weight.shape
    units = hidden_units // S
    fill = ((0, 0), (0, LANES - groups))
    high = lax.reduce_precision(weighting, 8, 7)
    low = weighting - high
    extended = jnp.concatenate(
        [tokens, jnp.pad(high, fill).astype(jnp.bfloat16), jnp.pad(low, fill).astype(jnp.bfloat16)], axis=1)
    wide = width + 2 * LANES
    bf = jnp.bfloat16
    hc = cols // 2
    group_rows = 2 * A * rows
    dma = pltpu.SemaphoreType.DMA
    scratch = [
        pltpu.VMEM((rows, wide), bf),
        pltpu.VMEM((B, group_rows, wide), bf),
        pltpu.VMEM((2 * units, width), bf),
        pltpu.VMEM((hidden_units, cols), bf),
        pltpu.VMEM((B, S, group_rows, units), bf),
        pltpu.VMEM((B, group_rows, cols), bf),
        pltpu.VMEM((B, group_rows, hc), bf),
        pltpu.VMEM((B, group_rows, hc), bf),
        pltpu.VMEM((B, group_rows, hc), bf),
        pltpu.VMEM((A, 2 * rows, hc), bf),
        pltpu.VMEM((A, 2 * rows, hc), bf),
        pltpu.VMEM((rows, hc), bf),
        pltpu.VMEM((rows, hc), bf),
        dma((3,)), dma, dma, dma((A,)), dma((A,)), dma((B, A)), dma((B, A)), dma((B, A)), dma((B, A)),
        dma((B, S)), dma((B, S)), dma((B,)), dma((B,)), dma((B, A)), dma((B, A)), dma((A,)), dma((A,)), dma, dma,
    ]
    return pl.pallas_call(
        functools.partial(moe_kernel, A, B, S, rows, width),
        out_shape=jax.ShapeDtypeStruct((rows, cols), bf),
        in_specs=[pl.BlockSpec(memory_space=pltpu.VMEM)] + [pl.BlockSpec(memory_space=pl.ANY)] * 3,
        out_specs=pl.BlockSpec(memory_space=pltpu.VMEM),
        scratch_shapes=scratch,
        compiler_params=pltpu.CompilerParams(
            collective_id=0, has_side_effects=True, vmem_limit_bytes=60 * 1024 * 1024),
    )(extended, gate_up, down_weight, new_rows)


def shards(
    tokens,
    expert_ids,
    route_weights,
    partner,
    gate_up,
    down_weight,
    down_grad,
    moment_one,
    moment_two,
):
    groups = lax.axis_size("expert")
    trained = down_grad.shape[1]
    new_rows, first_new, second_new = adamw(
        down_weight[:, :trained], down_grad, moment_one, moment_two
    )
    experts = jnp.arange(groups, dtype=jnp.int32)
    picked = expert_ids[:, :, None] == experts[None, None, :]
    weighting = jnp.sum(jnp.where(picked, route_weights[:, :, None], 0.0), axis=1)
    combined = experts_layer(
        tokens, weighting, gate_up.reshape(-1, gate_up.shape[3]), down_weight[0], new_rows[0]
    )
    wide = jnp.concatenate(
        [new_rows, first_new.astype(jnp.bfloat16), second_new.astype(jnp.bfloat16)], axis=0
    )
    arrived = relocate(wide, partner)
    rows_out = arrived[0:1]
    first_out = arrived[1:2].astype(jnp.float32)
    second_out = arrived[2:3].astype(jnp.float32)
    return (combined, rows_out, first_out, second_out)


def solution(mesh):
    return jax.shard_map(
        shards,
        mesh=mesh,
        in_specs=(
            P("expert", None),
            P("expert", None),
            P("expert", None),
            P(),
            P("expert", None, "shard", None),
            P("expert", None, "shard"),
            P("expert", None, "shard"),
            P("expert", None, "shard"),
            P("expert", None, "shard"),
        ),
        out_specs=(
            P("expert", "shard"),
            P("expert", None, "shard"),
            P("expert", None, "shard"),
            P("expert", None, "shard"),
        ),
        check_vma=False,
    )
```

```python
import functools

import jax
import jax.numpy as jnp
from jax import lax
from jax.experimental import pallas as pl
from jax.experimental.pallas import tpu as pltpu
from jax.sharding import PartitionSpec as P

STEP = 100


learn_rate = 0.01
beta_one = 0.9
beta_two = 0.999
epsilon = 1e-08
decay_rate = 0.1


def adamw(weight, gradient, first, second):
    grad_wide = gradient.astype(jnp.float32)
    first_new = beta_one * first + (1.0 - beta_one) * grad_wide
    second_new = beta_two * second + (1.0 - beta_two) * grad_wide * grad_wide
    first_hat = first_new / (1.0 - beta_one**STEP)
    second_hat = second_new / (1.0 - beta_two**STEP)
    weight_wide = weight.astype(jnp.float32)
    updated = weight_wide - learn_rate * (
        first_hat / (jnp.sqrt(second_hat) + epsilon) + decay_rate * weight_wide
    )
    return (updated.astype(jnp.bfloat16), first_new, second_new)


def relocate(payload, partner):
    groups = lax.axis_size("expert")
    me = lax.axis_index("expert")

    def exchange(distance):
        pairs = [(i, i ^ distance) for i in range(groups)]
        return lambda block: lax.ppermute(block, "expert", pairs)

    offset = lax.bitwise_xor(me, partner[me])
    return lax.switch(offset - 1, [exchange(d) for d in range(1, groups)], payload)


MESH_ID = pl.DeviceIdType.MESH
LANES = 128


def moe_kernel(A, B, S, rows, width, tok_ref, gate_ref, down_ref, new_ref, out_ref,
               slab, tok, gate, down, hid, part, got_core, acc, got_b, fin_in, got_a, tail_out, tail_in,
               local_sem, slab_s, slab_r, a_s, a_r, b_s, b_r, c_s, c_r, h_s, h_r,
               m_s, m_r, pc_s, pc_r, pb_s, pb_r, pa_s, pa_r, t_s, t_r):
    e = lax.axis_index("expert")
    y = lax.axis_index("shard")
    c = lax.rem(e, 2)
    chip = e // 2
    b = lax.rem(chip, B)
    a = chip // B
    quarter = tok.shape[2] // 4
    lane = lax.rem(y, 2)
    pair = 2 * rows
    units = hid.shape[3]
    cols = part.shape[2]
    hc = cols // 2
    trained = new_ref.shape[0]

    def expert_of(a1, b1, c1):
        return (a1 * B + b1) * 2 + c1

    def send(src, dst, ss, rs, target):
        copy = pltpu.make_async_remote_copy(
            src_ref=src, dst_ref=dst, send_sem=ss, recv_sem=rs,
            device_id=target, device_id_type=MESH_ID)
        copy.start()
        return copy

    def landed(dst, rs):
        pltpu.make_async_remote_copy(
            src_ref=dst, dst_ref=dst, send_sem=rs, recv_sem=rs,
            device_id=(expert_of(a, b, 1 - c), y), device_id_type=MESH_ID).wait_recv()

    loads = [
        pltpu.make_async_copy(gate_ref, gate, local_sem.at[0]),
        pltpu.make_async_copy(down_ref.at[pl.ds(trained, down.shape[0] - trained)],
                              down.at[pl.ds(trained, down.shape[0] - trained)], local_sem.at[1]),
        pltpu.make_async_copy(new_ref, down.at[pl.ds(0, trained)], local_sem.at[2]),
    ]
    for load in loads:
        load.start()

    core_dev = (expert_of(a, b, 1 - c), y)
    a_dev = [None] + [(expert_of(lax.rem(a + k, A), b, c), y) for k in range(1, A)]
    b_dev = [None] + [(expert_of(a, lax.rem(b + k, B), c), y) for k in range(1, B)]
    s_dev = [None] + [(e, lax.rem(y + k, S)) for k in range(1, S)]
    barrier = pltpu.get_barrier_semaphore()
    everyone = [core_dev] + a_dev[1:] + b_dev[1:] + s_dev[1:]
    for dev in everyone:
        pl.semaphore_signal(barrier, inc=1, device_id=dev, device_id_type=MESH_ID)
    pl.semaphore_wait(barrier, len(everyone))

    pending = [send(tok_ref, slab, slab_s, slab_r, core_dev)]
    landed(slab, slab_r)
    mine = tok_ref[...].astype(jnp.float32)
    other = slab[...].astype(jnp.float32)
    first = c == 0
    block = jnp.concatenate([jnp.where(first, mine, other), jnp.where(first, other, mine)], axis=0)

    def block_rows(k):
        return pl.ds(pl.multiple_of(lax.rem(a + k, A) * pair, 16), pair)

    def cols_of(core, part_lane):
        return pl.ds(pl.multiple_of((core * 2 + part_lane) * quarter, LANES), quarter)

    tok[b, block_rows(0), :] = block.astype(jnp.bfloat16)

    own = tok.at[b, block_rows(0), cols_of(c, lane)]
    for j in range(1, B):
        pending.append(send(own, own, b_s.at[j, 0], b_r.at[j, 0], b_dev[j]))
    for k in range(1, A):
        pending.append(send(own, own, a_s.at[k], a_r.at[k], a_dev[k]))
    mate_dev = (e, y + 1 - 2 * lane)

    def block_of(j, k, cols_there):
        return tok.at[lax.rem(b + B - j, B), block_rows(A - k), cols_there]

    def spread(j, k):
        piece = block_of(j, k, cols_of(c, lane))
        pending.append(send(piece, piece, m_s.at[j, k], m_r.at[j, k], mate_dev))
        pending.append(send(piece, piece, c_s.at[j, k, 0], c_r.at[j, k, 0], core_dev))

    def from_a(k):
        piece = block_of(0, k, cols_of(c, lane))
        landed(piece, a_r.at[k])
        for j in range(1, B):
            pending.append(send(piece, piece, b_s.at[j, k], b_r.at[j, k], b_dev[j]))
        spread(0, k)

    def from_b(j, k):
        landed(block_of(j, k, cols_of(c, lane)), b_r.at[j, k])
        spread(j, k)

    def collect(j, blocks):
        for k in blocks:
            piece = block_of(j, k, cols_of(c, 1 - lane))
            landed(piece, m_r.at[j, k])
            pending.append(send(piece, piece, c_s.at[j, k, 1], c_r.at[j, k, 1], core_dev))
        for k in blocks:
            landed(block_of(j, k, cols_of(1 - c, lane)), c_r.at[j, k, 0])
            landed(block_of(j, k, cols_of(1 - c, 1 - lane)), c_r.at[j, k, 1])

    for k in range(1, A):
        from_a(k)
        for j in range(1, B):
            from_b(j, k - 1)
    collect(0, range(1, A))
    for load in loads:
        load.wait()

    def project(j):
        bj = lax.rem(b + B - j, B)
        x = tok[bj, :, :width]
        both = lax.dot_general(x, gate[...], (((1,), (1,)), ((), ())), preferred_element_type=jnp.float32)
        g = both[:, :units]
        hid[bj, y] = (g / (1.0 + jnp.exp(-g)) * both[:, units:]).astype(jnp.bfloat16)
        piece = hid.at[bj, y]
        for s in range(1, S):
            pending.append(send(piece, piece, h_s.at[j, s], h_r.at[j, s], s_dev[s]))

    def finish(j):
        bj = lax.rem(b + B - j, B)
        for s in range(1, S):
            landed(hid.at[bj, lax.rem(y + S - s, S)], h_r.at[j, s])
        total = jnp.dot(hid[bj, 0], down[pl.ds(0, units), :], preferred_element_type=jnp.float32)
        for s in range(1, S):
            total += jnp.dot(hid[bj, s], down[pl.ds(s * units, units), :], preferred_element_type=jnp.float32)
        lanes = lax.broadcasted_iota(jnp.int32, (A * pair, LANES), 1)
        high = tok[bj, :, width:width + LANES].astype(jnp.float32)
        low = tok[bj, :, width + LANES:width + 2 * LANES].astype(jnp.float32)
        weight = jnp.sum(jnp.where(lanes == e, high + low, 0.0), axis=1, keepdims=True)
        part[bj] = (total * weight).astype(jnp.bfloat16)
        pending.append(send(part.at[bj, :, pl.ds(pl.multiple_of((1 - c) * hc, LANES), hc)],
                            got_core.at[bj], pc_s.at[j], pc_r.at[j], core_dev))

    def join(j):
        bj = lax.rem(b + B - j, B)
        landed(got_core.at[bj], pc_r.at[j])
        acc[j] = (part[bj, :, pl.ds(pl.multiple_of(c * hc, LANES), hc)].astype(jnp.float32)
                  + got_core[bj].astype(jnp.float32)).astype(jnp.bfloat16)
        if j:
            for k in range(A):
                src = acc.at[j, block_rows((k + 1) % A)]
                dst = got_b.at[j, block_rows((k + 1) % A)]
                pending.append(send(src, dst, pb_s.at[j, k], pb_r.at[j, k], b_dev[B - j]))

    project(0)
    for j in range(1, B):
        from_b(j, A - 1)
        if j == 1:
            finish(0)
        collect(j, range(A))
        project(j)
        if j == 1:
            join(0)
        finish(j)
        join(j)
    final = None
    for k in range(A):
        where = block_rows((k + 1) % A)
        total = acc[0, where, :].astype(jnp.float32)
        for j in range(1, B):
            landed(got_b.at[j, where], pb_r.at[j, k])
            total += got_b[j, where, :].astype(jnp.float32)
        if k < A - 1:
            fin_in[k + 1] = total.astype(jnp.bfloat16)
            pending.append(send(fin_in.at[k + 1], got_a.at[k + 1], pa_s.at[k + 1], pa_r.at[k + 1], a_dev[k + 1]))
        else:
            final = total
    for k in range(1, A):
        landed(got_a.at[k], pa_r.at[k])
        final += got_a[k].astype(jnp.float32)
    low_rows, high_rows = final[:rows], final[rows:]
    tail_out[...] = jnp.where(first, high_rows, low_rows).astype(jnp.bfloat16)
    pending.append(send(tail_out, tail_in, t_s, t_r, core_dev))
    out_ref[:, pl.ds(pl.multiple_of(c * hc, LANES), hc)] = jnp.where(first, low_rows, high_rows).astype(jnp.bfloat16)
    landed(tail_in, t_r)
    out_ref[:, pl.ds(pl.multiple_of((1 - c) * hc, LANES), hc)] = tail_in[...]
    for copy in pending:
        copy.wait_send()


def experts_layer(tokens, weighting, gate_up, down_weight, new_rows):
    groups = lax.axis_size("expert")
    S = lax.axis_size("shard")
    rows, width = tokens.shape
    B = groups // 8
    A = 4
    hidden_units, cols = down_weight.shape
    units = hidden_units // S
    fill = ((0, 0), (0, LANES - groups))
    high = lax.reduce_precision(weighting, 8, 7)
    low = weighting - high
    extended = jnp.concatenate(
        [tokens, jnp.pad(high, fill).astype(jnp.bfloat16), jnp.pad(low, fill).astype(jnp.bfloat16),
         jnp.zeros((rows, 2 * LANES), jnp.bfloat16)], axis=1)
    wide = width + 4 * LANES
    bf = jnp.bfloat16
    hc = cols // 2
    group_rows = 2 * A * rows
    dma = pltpu.SemaphoreType.DMA
    scratch = [
        pltpu.VMEM((rows, wide), bf),
        pltpu.VMEM((B, group_rows, wide), bf),
        pltpu.VMEM((2 * units, width), bf),
        pltpu.VMEM((hidden_units, cols), bf),
        pltpu.VMEM((B, S, group_rows, units), bf),
        pltpu.VMEM((B, group_rows, cols), bf),
        pltpu.VMEM((B, group_rows, hc), bf),
        pltpu.VMEM((B, group_rows, hc), bf),
        pltpu.VMEM((B, group_rows, hc), bf),
        pltpu.VMEM((A, 2 * rows, hc), bf),
        pltpu.VMEM((A, 2 * rows, hc), bf),
        pltpu.VMEM((rows, hc), bf),
        pltpu.VMEM((rows, hc), bf),
        dma((3,)), dma, dma, dma((A,)), dma((A,)), dma((B, A)), dma((B, A)), dma((B, A, 2)), dma((B, A, 2)),
        dma((B, S)), dma((B, S)), dma((B, A)), dma((B, A)), dma((B,)), dma((B,)), dma((B, A)), dma((B, A)), dma((A,)), dma((A,)), dma, dma,
    ]
    return pl.pallas_call(
        functools.partial(moe_kernel, A, B, S, rows, width),
        out_shape=jax.ShapeDtypeStruct((rows, cols), bf),
        in_specs=[pl.BlockSpec(memory_space=pltpu.VMEM)] + [pl.BlockSpec(memory_space=pl.ANY)] * 3,
        out_specs=pl.BlockSpec(memory_space=pltpu.VMEM),
        scratch_shapes=scratch,
        compiler_params=pltpu.CompilerParams(
            collective_id=0, has_side_effects=True, vmem_limit_bytes=60 * 1024 * 1024),
    )(extended, gate_up, down_weight, new_rows)


def shards(
    tokens,
    expert_ids,
    route_weights,
    partner,
    gate_up,
    down_weight,
    down_grad,
    moment_one,
    moment_two,
):
    groups = lax.axis_size("expert")
    trained = down_grad.shape[1]
    new_rows, first_new, second_new = adamw(
        down_weight[:, :trained], down_grad, moment_one, moment_two
    )
    experts = jnp.arange(groups, dtype=jnp.int32)
    picked = expert_ids[:, :, None] == experts[None, None, :]
    weighting = jnp.sum(jnp.where(picked, route_weights[:, :, None], 0.0), axis=1)
    combined = experts_layer(
        tokens, weighting, gate_up.reshape(-1, gate_up.shape[3]), down_weight[0], new_rows[0]
    )
    wide = jnp.concatenate(
        [new_rows, first_new.astype(jnp.bfloat16), second_new.astype(jnp.bfloat16)], axis=0
    )
    arrived = relocate(wide, partner)
    rows_out = arrived[0:1]
    first_out = arrived[1:2].astype(jnp.float32)
    second_out = arrived[2:3].astype(jnp.float32)
    return (combined, rows_out, first_out, second_out)


def solution(mesh):
    return jax.shard_map(
        shards,
        mesh=mesh,
        in_specs=(
            P("expert", None),
            P("expert", None),
            P("expert", None),
            P(),
            P("expert", None, "shard", None),
            P("expert", None, "shard"),
            P("expert", None, "shard"),
            P("expert", None, "shard"),
            P("expert", None, "shard"),
        ),
        out_specs=(
            P("expert", "shard"),
            P("expert", None, "shard"),
            P("expert", None, "shard"),
            P("expert", None, "shard"),
        ),
        check_vma=False,
    )
```
